32 devices in a mesh: dp: 2 (over x), expert: 4 (over z), mp: 4 (over y, core).
Axes of the slice: x: 2, y: 2, z: 4, core: 2. Of those that a mesh axis runs over, the one named last changes fastest.
Arguments:
- tokens: bfloat16 [1024, 3072], P(('dp', 'expert'), 'mp'), may hold values from -6 to 6
- expert_ids: int32 [1024, 2], P(('dp', 'expert')), may hold values from 0 to 3, all different within a row; in each aligned block of 128 rows (0 to 127, 128 to 255, ...) at most 72 rows name the same one
- route_weight: bfloat16 [1024, 2], P(('dp', 'expert')), may hold values from 0.099609375 to 1
- w_gate: bfloat16 [4, 3072, 8192], P(None, ('dp', 'expert'), 'mp'), may hold values from -0.109375 to 0.109375
- w_up: bfloat16 [4, 3072, 8192], P(None, ('dp', 'expert'), 'mp'), may hold values from -0.109375 to 0.109375
- grad_hidden: bfloat16 [4, 2, 4, 72, 8192], P('expert', 'dp', None, None, 'mp'), may hold values from -6 to 6
Outputs:
- hidden_out: bfloat16 [4, 2, 4, 72, 8192], P('expert', 'dp', None, None, 'mp')
- grad_tokens: bfloat16 [1024, 3072], P(('dp', 'expert'), 'mp')
The draws below stay inside these ranges and needn't reach their ends.
Inputs may be any that keep to these rules, and one draw needn't show every extreme that they name: `expert_ids`: each row names 2 different experts; among the rows of one token group no expert is named more than 72 times, a bound that some block reaches.
All inputs are finite; a program needn't handle non-finite values.
Results may differ from the reference program's by a relative error of at most 0.0049.
Values may be sent and summed in bfloat16 or wider, within the bound.
No kernel may reach another device: no remote copies, remote signals or barrier semaphores. Data moves between devices by JAX's collectives and lax.ppermute only.
A program may use at most 128 MiB of HBM per device.

```python
import math
import jax
import jax.numpy as jnp
import numpy as np
from jax import lax

D = 3072
FF = 8192
TOP = 2
TOK_GRP = 128
E = 4
C = 72
TOKENS = 1024
N_DP = 2
N_EXPERT = 4


def steps_of(rng, shape, cuts, smallest, largest):
    level, own = 1.0, jax.random.fold_in(rng, 6)
    for dim, blocks in cuts:
        heights = jnp.exp(jax.random.uniform(jax.random.fold_in(own, dim), (blocks,), jnp.float32, smallest / len(cuts), largest / len(cuts)))
        level = level * jnp.repeat(heights, shape[dim] // blocks).reshape([-1 if axis == dim else 1 for axis in range(len(shape))])
    return level


def shared_out(rng, own, number, rows, amount, top, limit, lean):
    order = jax.random.permutation(rng, amount)
    packed, ordinary = shares(amount, rows * top, limit, lean, True), shares(amount, rows * top, limit, lean, False)
    places = jnp.arange(amount)

    def named(tallies, rotation):
        used = int((tallies > 0).sum())
        fixed = max(1, used // 4)
        passed = fixed + (places - fixed + rotation * (used - fixed)) % max(1, amount - fixed)
        return jnp.zeros((amount,), jnp.int32).at[order[jnp.where(places < fixed, places, passed)]].set(jnp.asarray(tallies, jnp.int32))

    tallies = jnp.where(number % 4 == 0, named(packed, number // 4), named(ordinary, number - number // 4 - 1))
    mixed = jax.random.permutation(jax.random.fold_in(own, 3), amount)
    giver, receiver = mixed[0:amount // 2 * 2:2], mixed[1:amount // 2 * 2:2]
    slack = jnp.minimum(tallies[giver] - 1, limit - tallies[receiver]) // 2
    slack = jnp.where((giver == order[0]) | (receiver == order[0]) | (tallies[receiver] == 0), 0, jnp.maximum(slack, 0))
    passed = jax.random.randint(jax.random.fold_in(own, 4), (amount // 2,), 0, 1 << 20) % (slack + 1)
    tallies = tallies.at[giver].add(-passed).at[receiver].add(passed)
    labels = jnp.searchsorted(jnp.cumsum(tallies), jnp.arange(rows * top), side="right").astype(jnp.int32)
    listing = labels.reshape(top, rows).T
    listing = listing[jax.random.permutation(jax.random.fold_in(own, 1), rows)]
    rotation = jax.random.randint(jax.random.fold_in(own, 2), (rows, 1), 0, top)
    return jnp.take_along_axis(listing, (jnp.arange(top)[None, :] + rotation) % top, axis=1)


def shares(count, total, most, slope, full):
    weights = [(1 << 20) // math.isqrt(grade ** slope) + 1 for grade in range(1, count + 1)]
    largest = most if full else min(most, max(-(-total // count), total * weights[0] // sum(weights)))
    least = 1 if total - largest >= count - 1 else 0
    holding, spare = [largest] + [least] * (count - 1), total - largest - least * (count - 1)
    while spare > 0:
        free = [i for i in range(1, count) if holding[i] < largest] or [i for i in range(1, count) if holding[i] < most]
        whole, budget = sum([weights[i] for i in free]), spare
        for i in free:
            more = min(most - holding[i], max(1, budget * weights[i] // whole), spare)
            holding[i] = holding[i] + more
            spare = spare - more
    return np.array(holding)


def centred(key, shape, scale, most, pieces=(), kind=jnp.bfloat16):
    entries = scale * jax.random.normal(key, shape, jnp.float32)
    if pieces:
        entries = entries * steps_of(key, shape, pieces, -0.22, 0.18)
    return jnp.clip(entries, -most, most).astype(kind)


def setup_inputs(seed: int = 0) -> dict:
    seeds = jax.random.split(jax.random.key(seed), 7)
    tokens = centred(seeds[0], (TOKENS, D), 1.0, 6.0, ((0, 8), (1, 4)))
    expert_ids_keys = jax.random.split(jax.random.fold_in(seeds[1], 1), TOKENS // TOK_GRP)
    expert_ids_turns = jax.random.permutation(jax.random.fold_in(seeds[1], 3), TOKENS // TOK_GRP)
    expert_ids = jax.vmap(lambda own, number: shared_out(jax.random.fold_in(seeds[1], 2), own, number, TOK_GRP, E, TOP, C, 1))(expert_ids_keys, expert_ids_turns).reshape((TOKENS, TOP))
    route_weight = jnp.clip(jnp.exp(math.log(1.0) - 2.306499 * jax.random.uniform(seeds[2], (TOKENS, TOP), jnp.float32) ** steps_of(seeds[2], (TOKENS, TOP), ((0, 8),), -0.2, 0.2)), 0.099609375, 1.0).astype(jnp.bfloat16)
    w_gate = centred(seeds[3], (E, D, FF), D ** -0.5, 0.109375, ((1, 8), (2, 4)))
    w_up = centred(seeds[4], (E, D, FF), D ** -0.5, 0.109375, ((1, 8), (2, 4)))
    grad_hidden = centred(seeds[5], (E, N_DP, N_EXPERT, C, FF), 1.0, 6.0, ((0, 4), (1, 2), (4, 4)))
    return {"tokens": tokens, "expert_ids": expert_ids, "route_weight": route_weight, "w_gate": w_gate, "w_up": w_up, "grad_hidden": grad_hidden}


def slot_map(expert_ids):
    flat_ids = expert_ids.reshape(-1)
    onehot = (flat_ids[:, None] == jnp.arange(E, dtype=jnp.int32)[None, :]).astype(jnp.int32)
    before = jnp.cumsum(onehot, axis=0) - onehot
    position = jnp.sum(before * onehot, axis=1)
    target = flat_ids * C + position
    placed = target[:, None] == jnp.arange(E * C, dtype=jnp.int32)[None, :]
    return placed.reshape(expert_ids.shape[0], expert_ids.shape[1], E * C)


def expert_pass(inputs):
    slot_rows, slot_scale, gate_w, up_w, grad = inputs
    gate_value = jnp.dot(slot_rows, gate_w, preferred_element_type=jnp.float32)
    up_value = jnp.dot(slot_rows, up_w, preferred_element_type=jnp.float32)
    sigmoid_gate = jax.nn.sigmoid(gate_value)
    weight = slot_scale.astype(jnp.float32)[:, None]
    hidden = (weight * gate_value * sigmoid_gate * up_value).astype(jnp.bfloat16)
    grad_act = weight * grad.astype(jnp.float32)
    gate_grad = (grad_act * up_value * sigmoid_gate * (1.0 + gate_value * (1.0 - sigmoid_gate))).astype(jnp.bfloat16)
    up_grad = (grad_act * gate_value * sigmoid_gate).astype(jnp.bfloat16)
    dims = (((1,), (1,)), ((), ()))
    back_term = lax.dot_general(gate_grad, gate_w, dims, preferred_element_type=jnp.float32)
    back_term = back_term + lax.dot_general(up_grad, up_w, dims, preferred_element_type=jnp.float32)
    return hidden, back_term


def reference(tokens, expert_ids, route_weight, w_gate, w_up, grad_hidden):
    groups = N_DP * N_EXPERT
    tok_blocks = tokens.reshape(groups, TOK_GRP, D).astype(jnp.float32)
    id_blocks = expert_ids.reshape(groups, TOK_GRP, TOP)
    weight_blocks = route_weight.reshape(groups, TOK_GRP, TOP).astype(jnp.float32)
    placed = jax.vmap(slot_map)(id_blocks).astype(jnp.float32)
    select = jnp.sum(placed, axis=2)
    sent_rows = jnp.einsum("gts,gtd->gsd", select, tok_blocks, precision=lax.Precision.HIGHEST).astype(jnp.bfloat16)
    sent_scale = jnp.einsum("gtks,gtk->gs", placed, weight_blocks, precision=lax.Precision.HIGHEST).astype(jnp.bfloat16)
    rows_expert = sent_rows.reshape(groups, E, C, D).transpose(1, 0, 2, 3).reshape(E, groups * C, D)
    scale_expert = sent_scale.reshape(groups, E, C).transpose(1, 0, 2).reshape(E, groups * C)
    grad_expert = grad_hidden.reshape(E, groups * C, FF)
    hidden, back_term = lax.map(expert_pass, (rows_expert, scale_expert, w_gate, w_up, grad_expert))
    hidden_out = hidden.reshape(E, N_DP, N_EXPERT, C, FF)
    back_groups = back_term.reshape(E, groups, C, D).transpose(1, 0, 2, 3).reshape(groups, E * C, D)
    grad_blocks = jnp.einsum("gts,gsd->gtd", select, back_groups, precision=lax.Precision.HIGHEST)
    grad_tokens = grad_blocks.reshape(TOKENS, D).astype(jnp.bfloat16)
    return hidden_out, grad_tokens
```

```python
import functools

import jax
import jax.numpy as jnp
from jax import lax
from jax.experimental import pallas as pl
from jax.experimental.pallas import tpu as pltpu
from jax.sharding import PartitionSpec as P

Z_WINDOW = 3
X_WINDOW = 3
Z_LAG = 3
X_LAG = 2
OWN_AT = (0, 0, 0, 1, 2, 3, 4, 5)
NT = (((1,), (1,)), ((), ()))


def slot_map(expert_ids, n_expert, slots_cap):
    flat_ids = expert_ids.reshape(-1)
    onehot = (flat_ids[:, None] == jnp.arange(n_expert, dtype=jnp.int32)[None, :]).astype(jnp.int32)
    before = jnp.cumsum(onehot, axis=0) - onehot
    position = jnp.sum(before * onehot, axis=1)
    target = flat_ids * slots_cap + position
    placed = target[:, None] == jnp.arange(n_expert * slots_cap, dtype=jnp.int32)[None, :]
    return placed.reshape(expert_ids.shape[0], expert_ids.shape[1], n_expert * slots_cap)


def shift_by(axis, step):
    size = lax.axis_size(axis)
    return [(source, (source + step) % size) for source in range(size)]


def exchange(axis, bit):
    return [(source, source ^ bit) for source in range(lax.axis_size(axis))]


def after(value, *others):
    return lax.optimization_barrier((value, *others))[0]


def column_chunks(width):
    unit = width // 16
    sizes = (2, 4, 4, 4, 2)
    bounds = [0]
    for size in sizes:
        bounds.append(bounds[-1] + size * unit)
    return list(zip(bounds[:-1], bounds[1:]))


def expert_kernel(n_part, first, rows_ref, scale_ref, grad_ref, *refs):
    parts, rest = refs[:n_part], refs[n_part:]
    if first:
        hidden_ref, back_ref, done_ref = rest
    else:
        back_in, _, hidden_ref, back_ref, done_ref = rest
    depth = parts[0].shape[1]

    @pl.when(pl.program_id(0) == 0)
    def _():
        if first:
            back_ref[...] = jnp.zeros_like(back_ref)
        else:
            back_ref[...] = back_in[...]
        done_ref[...] = jnp.zeros_like(done_ref)

    gate = up = None
    for index, part in enumerate(parts):
        rows = rows_ref[:, index * depth : (index + 1) * depth]
        gate_term = jnp.dot(rows, part[0], preferred_element_type=jnp.float32)
        up_term = jnp.dot(rows, part[1], preferred_element_type=jnp.float32)
        gate = gate_term if gate is None else gate + gate_term
        up = up_term if up is None else up + up_term
    weight = scale_ref[...]
    sig = jax.nn.sigmoid(gate)
    hidden_ref[...] = (weight * gate * sig * up).astype(jnp.bfloat16)
    grad_act = weight * grad_ref[...].astype(jnp.float32)
    gate_grad = (grad_act * up * sig * (1.0 + gate * (1.0 - sig))).astype(jnp.bfloat16)
    up_grad = (grad_act * gate * sig).astype(jnp.bfloat16)
    for index, part in enumerate(parts):
        columns = slice(index * depth, (index + 1) * depth)
        back_ref[:, columns] += lax.dot_general(
            gate_grad, part[0], NT, preferred_element_type=jnp.float32
        ) + lax.dot_general(up_grad, part[1], NT, preferred_element_type=jnp.float32)


def expert_chunk(rows, scale, grad, parts, begin, carried):
    slot_count, width_all = rows.shape
    hidden_part = grad.shape[1]
    depth, width = parts[0].shape[1:]
    tile = 256 if width % 256 == 0 and begin % 256 == 0 else 128
    tile = tile if width % tile == 0 else width
    offset = begin // tile
    whole = lambda shape: pl.BlockSpec(shape, lambda t: (0, 0))
    columns = pl.BlockSpec((slot_count, tile), lambda t: (0, offset + t))
    in_specs = [whole((slot_count, width_all)), whole((slot_count, 1)), columns]
    in_specs += [pl.BlockSpec((2, depth, tile), lambda t: (0, 0, t))] * len(parts)
    operands = [rows, scale, grad, *parts]
    aliases = {}
    if carried is not None:
        hidden, back = carried
        in_specs += [whole((slot_count, width_all)), pl.BlockSpec(memory_space=pl.ANY)]
        aliases = {len(operands): 1, len(operands) + 1: 0}
        operands += [back, hidden]
    return pl.pallas_call(
        functools.partial(expert_kernel, len(parts), carried is None),
        grid=(width // tile,),
        out_shape=(
            jax.ShapeDtypeStruct((slot_count, hidden_part), jnp.bfloat16),
            jax.ShapeDtypeStruct((slot_count, width_all), jnp.float32),
            jax.ShapeDtypeStruct((8, 128), jnp.float32),
        ),
        in_specs=in_specs,
        out_specs=(columns, whole((slot_count, width_all)), whole((8, 128))),
        input_output_aliases=aliases,
        compiler_params=pltpu.CompilerParams(vmem_limit_bytes=48 * 1024 * 1024),
        cost_estimate=pl.CostEstimate(
            flops=8 * slot_count * width_all * width,
            bytes_accessed=4 * width_all * width + 10 * slot_count * width_all,
            transcendentals=slot_count * width,
        ),
    )(*operands)


def per_device(tokens, expert_ids, route_weight, w_gate, w_up, grad_hidden):
    n_expert = lax.axis_size("expert")
    n_dp = lax.axis_size("dp")
    n_mp = lax.axis_size("mp")
    my_expert = lax.axis_index("expert")
    my_dp = lax.axis_index("dp")
    my_mp = lax.axis_index("mp")
    slots_cap = grad_hidden.shape[3]
    feat_part = tokens.shape[1]
    depth = w_gate.shape[1]
    hidden_part = w_gate.shape[2]
    slot_count = n_expert * slots_cap
    width_all = n_expert * n_dp * depth
    chunks = column_chunks(hidden_part)
    pair = n_dp == 2

    def stored(chunk, step):
        begin, end = chunks[chunk]
        target = lax.rem(my_expert + step, n_expert)
        return jnp.stack(
            [
                lax.dynamic_slice(w, (target, 0, begin), (1, depth, end - begin))[0]
                for w in (w_gate, w_up)
            ]
        )

    shifts = sorted(range(1, n_expert), key=lambda s: -abs(2 * s - n_expert))
    landed, arrivals = {}, []
    spread, crossings = {}, []
    carried, finished = None, []

    def to_owner(chunk, step):
        piece = stored(chunk, step)
        if step:
            first = [arrivals[-Z_WINDOW]] if len(arrivals) >= Z_WINDOW else []
            if chunk >= Z_LAG:
                first.append(finished[chunk - Z_LAG])
            if first:
                piece = after(piece, *first)
            piece = lax.ppermute(piece, "expert", shift_by("expert", step))
            arrivals.append(piece)
        landed[chunk, step] = piece

    def to_both(chunk, step):
        piece = landed[chunk, step]
        first = [crossings[-X_WINDOW]] if len(crossings) >= X_WINDOW else []
        if step and chunk >= X_LAG:
            first.append(finished[chunk - X_LAG])
        if first:
            piece = after(piece, *first)
        if pair:
            spread[chunk, step] = lax.ppermute(piece, "dp", shift_by("dp", 1))
        else:
            spread[chunk, step] = lax.all_gather(piece, "dp", axis=1, tiled=True)
        crossings.append(spread[chunk, step])

    to_owner(0, 0)
    for step in shifts:
        to_owner(0, step)
    to_both(0, 0)

    def place_of(dp_index, expert_index):
        step = lax.rem(my_expert - expert_index + n_expert, n_expert)
        far = lax.rem(my_dp - dp_index + n_dp, n_dp) if pair else dp_index
        return (step * n_dp + far) * depth

    order = []
    for step in range(n_expert):
        expert_index = lax.rem(my_expert - step + n_expert, n_expert)
        for far in range(n_dp):
            dp_index = lax.rem(my_dp - far + n_dp, n_dp) if pair else far
            order.append((dp_index * n_expert + expert_index) * depth)

    expert_ids = after(expert_ids, landed[0, 0])
    placed = slot_map(expert_ids, n_expert, slots_cap).astype(jnp.float32)
    select = jnp.sum(placed, axis=1)
    sent_rows = jnp.dot(
        select.T.astype(jnp.bfloat16), tokens, preferred_element_type=jnp.float32
    ).astype(jnp.bfloat16)
    sent_scale = jnp.einsum(
        "tks,tk->s", placed, route_weight.astype(jnp.float32), precision=lax.Precision.HIGHEST
    ).astype(jnp.bfloat16)
    sent = jnp.concatenate(
        [sent_rows, jnp.broadcast_to(sent_scale[:, None], (slot_count, 128))], axis=1
    ).reshape(n_expert, slots_cap, feat_part + 128)
    came = []
    for step in range(n_expert):
        block = lax.dynamic_index_in_dim(sent, lax.rem(my_expert + step, n_expert), 0, keepdims=False)
        came.append(lax.ppermute(block, "expert", shift_by("expert", step)) if step else block)
    came = jnp.stack(came)
    slots = jnp.concatenate(
        [
            lax.dynamic_index_in_dim(came, lax.rem(my_expert - group + n_expert, n_expert), 0, keepdims=False)
            for group in range(n_expert)
        ],
        axis=0,
    )
    scale = slots[:, feat_part : feat_part + 1].astype(jnp.float32)
    rows_full = lax.all_gather(slots[:, :feat_part], "mp", axis=1, tiled=True)
    rows = jnp.concatenate(
        [lax.dynamic_slice(rows_full, (0, start), (slot_count, depth)) for start in order], axis=1
    )
    grad_rows = grad_hidden.reshape(slot_count, hidden_part)

    n_chunk = len(chunks)
    own_at = OWN_AT
    for chunk in range(n_chunk):
        for later in range(1, n_chunk):
            if own_at[later] == chunk:
                to_owner(later, 0)
                to_both(later, 0)
        if chunk:
            for step in shifts:
                to_owner(chunk, step)
        for step in shifts:
            to_both(chunk, step)
        parts = []
        for step in range(n_expert):
            parts += [landed[chunk, step], spread[chunk, step]] if pair else [spread[chunk, step]]
        *carried, done = expert_chunk(rows, scale, grad_rows, parts, chunks[chunk][0], carried)
        finished.append(done)
    hidden, back = carried

    blocks_per_part = feat_part // depth

    def features(part_index):
        blocks = []
        for block in range(blocks_per_part):
            number = part_index * blocks_per_part + block
            start = place_of(number // n_expert, lax.rem(number, n_expert))
            blocks.append(lax.dynamic_slice(back, (0, start), (slot_count, depth)))
        return jnp.concatenate(blocks, axis=1)

    sums = {bits: features(my_mp ^ bits) for bits in range(n_mp)}
    bit = 1
    while 2 * bit < n_mp:
        going = [bits for bits in sums if bits & bit]
        got = lax.ppermute(jnp.stack([sums[bits] for bits in going]), "mp", exchange("mp", bit))
        for index, bits in enumerate(going):
            sums[bits ^ bit] = sums[bits ^ bit] + got[index]
            del sums[bits]
        bit *= 2
    kept = sums[0].reshape(n_expert, slots_cap, feat_part)
    given = sums[bit].reshape(n_expert, slots_cap, feat_part)
    returned = {}
    for step in sorted(range(n_expert), key=lambda s: abs(2 * s - n_expert) if s else 2 * n_expert):
        group = lax.rem(my_expert + step, n_expert)
        block = lax.dynamic_index_in_dim(given, group, 0, keepdims=False)
        block = lax.ppermute(block.astype(jnp.bfloat16), "mp", exchange("mp", bit))
        block = lax.dynamic_index_in_dim(kept, group, 0, keepdims=False) + block.astype(jnp.float32)
        block = block.astype(jnp.bfloat16)
        returned[step] = lax.ppermute(block, "expert", shift_by("expert", step)) if step else block
    split = select.reshape(select.shape[0], n_expert, slots_cap)
    chosen = jnp.concatenate(
        [
            lax.dynamic_index_in_dim(split, lax.rem(my_expert - step + n_expert, n_expert), 1, keepdims=False)
            for step in range(n_expert)
        ],
        axis=1,
    )
    grad_tokens = jnp.dot(
        chosen,
        jnp.concatenate([returned[step] for step in range(n_expert)], axis=0).astype(jnp.float32),
        precision=lax.Precision.HIGHEST,
    )
    hidden_out = hidden.reshape(1, 1, n_expert, slots_cap, hidden_part)
    return (hidden_out, grad_tokens.astype(jnp.bfloat16))


def solution(mesh):
    in_specs = (
        P(("dp", "expert"), "mp"),
        P(("dp", "expert"), None),
        P(("dp", "expert"), None),
        P(None, ("dp", "expert"), "mp"),
        P(None, ("dp", "expert"), "mp"),
        P("expert", "dp", None, None, "mp"),
    )
    out_specs = (P("expert", "dp", None, None, "mp"), P(("dp", "expert"), "mp"))
    return jax.shard_map(
        per_device, mesh=mesh, in_specs=in_specs, out_specs=out_specs, check_vma=False
    )
```

```python
import functools

import jax
import jax.numpy as jnp
from jax import lax
from jax.experimental import pallas as pl
from jax.experimental.pallas import tpu as pltpu
from jax.sharding import PartitionSpec as P

Z_WINDOW = 3
X_WINDOW = 3
Z_AFTER = {3: 0, 4: 1}
X_AFTER = {2: 0, 3: 1, 4: 2}
OWN_AT = (0, 0, 0, 1, 2, 3, 4, 5)
Y_PARTS = 2
NT = (((1,), (1,)), ((), ()))


def slot_map(expert_ids, n_expert, slots_cap):
    flat_ids = expert_ids.reshape(-1)
    onehot = (flat_ids[:, None] == jnp.arange(n_expert, dtype=jnp.int32)[None, :]).astype(jnp.int32)
    before = jnp.cumsum(onehot, axis=0) - onehot
    position = jnp.sum(before * onehot, axis=1)
    target = flat_ids * slots_cap + position
    placed = target[:, None] == jnp.arange(n_expert * slots_cap, dtype=jnp.int32)[None, :]
    return placed.reshape(expert_ids.shape[0], expert_ids.shape[1], n_expert * slots_cap)


def shift_by(axis, step):
    size = lax.axis_size(axis)
    return [(source, (source + step) % size) for source in range(size)]


def exchange(axis, bit):
    return [(source, source ^ bit) for source in range(lax.axis_size(axis))]


def after(value, *others):
    return lax.optimization_barrier((value, *others))[0]


def gather_rows(block):
    size = lax.axis_size("mp")
    me = lax.axis_index("mp")
    held = jnp.stack([block] + [lax.ppermute(block, "mp", exchange("mp", bits)) for bits in range(1, size)])
    return jnp.concatenate([lax.dynamic_index_in_dim(held, me ^ index, 0, keepdims=False) for index in range(size)], axis=1)


def column_chunks(width):
    unit = width // 16
    sizes = (3, 4, 4, 3, 2)
    bounds = [0]
    for size in sizes:
        bounds.append(bounds[-1] + size * unit)
    return list(zip(bounds[:-1], bounds[1:]))


def expert_kernel(n_part, first, rows_ref, scale_ref, grad_ref, *refs):
    parts, rest = refs[:n_part], refs[n_part:]
    if first:
        hidden_ref, back_ref, done_ref = rest
    else:
        back_in, _, hidden_ref, back_ref, done_ref = rest
    depth = parts[0].shape[1]

    @pl.when(pl.program_id(0) == 0)
    def _():
        if first:
            back_ref[...] = jnp.zeros_like(back_ref)
        else:
            back_ref[...] = back_in[...]
        done_ref[...] = jnp.zeros_like(done_ref)

    gate = up = None
    for index, part in enumerate(parts):
        rows = rows_ref[:, index * depth : (index + 1) * depth]
        gate_term = jnp.dot(rows, part[0], preferred_element_type=jnp.float32)
        up_term = jnp.dot(rows, part[1], preferred_element_type=jnp.float32)
        gate = gate_term if gate is None else gate + gate_term
        up = up_term if up is None else up + up_term
    weight = scale_ref[...]
    sig = jax.nn.sigmoid(gate)
    hidden_ref[...] = (weight * gate * sig * up).astype(jnp.bfloat16)
    grad_act = weight * grad_ref[...].astype(jnp.float32)
    gate_grad = (grad_act * up * sig * (1.0 + gate * (1.0 - sig))).astype(jnp.bfloat16)
    up_grad = (grad_act * gate * sig).astype(jnp.bfloat16)
    for index, part in enumerate(parts):
        columns = slice(index * depth, (index + 1) * depth)
        back_ref[:, columns] += lax.dot_general(
            gate_grad, part[0], NT, preferred_element_type=jnp.float32
        ) + lax.dot_general(up_grad, part[1], NT, preferred_element_type=jnp.float32)


def expert_chunk(rows, scale, grad, parts, begin, carried):
    slot_count, width_all = rows.shape
    hidden_part = grad.shape[1]
    depth, width = parts[0].shape[1:]
    tile = 256 if width % 256 == 0 and begin % 256 == 0 else 128
    tile = tile if width % tile == 0 else width
    offset = begin // tile
    whole = lambda shape: pl.BlockSpec(shape, lambda t: (0, 0))
    columns = pl.BlockSpec((slot_count, tile), lambda t: (0, offset + t))
    in_specs = [whole((slot_count, width_all)), whole((slot_count, 1)), columns]
    in_specs += [pl.BlockSpec((2, depth, tile), lambda t: (0, 0, t))] * len(parts)
    operands = [rows, scale, grad, *parts]
    aliases = {}
    if carried is not None:
        hidden, back = carried
        in_specs += [whole((slot_count, width_all)), pl.BlockSpec(memory_space=pl.ANY)]
        aliases = {len(operands): 1, len(operands) + 1: 0}
        operands += [back, hidden]
    return pl.pallas_call(
        functools.partial(expert_kernel, len(parts), carried is None),
        grid=(width // tile,),
        out_shape=(
            jax.ShapeDtypeStruct((slot_count, hidden_part), jnp.bfloat16),
            jax.ShapeDtypeStruct((slot_count, width_all), jnp.float32),
            jax.ShapeDtypeStruct((8, 128), jnp.float32),
        ),
        in_specs=in_specs,
        out_specs=(columns, whole((slot_count, width_all)), whole((8, 128))),
        input_output_aliases=aliases,
        compiler_params=pltpu.CompilerParams(vmem_limit_bytes=48 * 1024 * 1024),
        cost_estimate=pl.CostEstimate(
            flops=1024, bytes_accessed=1024, transcendentals=0,
        ),
    )(*operands)


def per_device(tokens, expert_ids, route_weight, w_gate, w_up, grad_hidden):
    n_expert = lax.axis_size("expert")
    n_dp = lax.axis_size("dp")
    n_mp = lax.axis_size("mp")
    my_expert = lax.axis_index("expert")
    my_dp = lax.axis_index("dp")
    my_mp = lax.axis_index("mp")
    slots_cap = grad_hidden.shape[3]
    feat_part = tokens.shape[1]
    depth = w_gate.shape[1]
    hidden_part = w_gate.shape[2]
    slot_count = n_expert * slots_cap
    width_all = n_expert * n_dp * depth
    chunks = column_chunks(hidden_part)
    pair = n_dp == 2

    def stored(chunk, step):
        begin, end = chunks[chunk]
        target = lax.rem(my_expert + step, n_expert)
        return jnp.stack(
            [
                lax.dynamic_slice(w, (target, 0, begin), (1, depth, end - begin))[0]
                for w in (w_gate, w_up)
            ]
        )

    shifts = sorted(range(1, n_expert), key=lambda s: -abs(2 * s - n_expert))
    landed, arrivals = {}, []
    spread, crossings = {}, []
    carried, finished = None, []

    def to_owner(chunk, step):
        piece = stored(chunk, step)
        if step:
            first = [arrivals[-Z_WINDOW]] if len(arrivals) >= Z_WINDOW else []
            if chunk in Z_AFTER:
                first.append(finished[Z_AFTER[chunk]])
            if first:
                piece = after(piece, *first)
            piece = lax.ppermute(piece, "expert", shift_by("expert", step))
            arrivals.append(piece)
        landed[chunk, step] = piece

    def to_both(chunk, step):
        piece = landed[chunk, step]
        first = [crossings[-X_WINDOW]] if len(crossings) >= X_WINDOW else []
        if step and chunk in X_AFTER:
            first.append(finished[X_AFTER[chunk]])
        if first:
            piece = after(piece, *first)
        if pair:
            spread[chunk, step] = lax.ppermute(piece, "dp", shift_by("dp", 1))
        else:
            spread[chunk, step] = lax.all_gather(piece, "dp", axis=1, tiled=True)
        crossings.append(spread[chunk, step])

    to_owner(0, 0)
    for step in shifts:
        to_owner(0, step)
    to_both(0, 0)

    def place_of(dp_index, expert_index):
        step = lax.rem(my_expert - expert_index + n_expert, n_expert)
        far = lax.rem(my_dp - dp_index + n_dp, n_dp) if pair else dp_index
        return (step * n_dp + far) * depth

    order = []
    for step in range(n_expert):
        expert_index = lax.rem(my_expert - step + n_expert, n_expert)
        for far in range(n_dp):
            dp_index = lax.rem(my_dp - far + n_dp, n_dp) if pair else far
            order.append((dp_index * n_expert + expert_index) * depth)

    placed = slot_map(expert_ids, n_expert, slots_cap).astype(jnp.float32)
    select = jnp.sum(placed, axis=1)
    sent_rows = jnp.dot(
        select.T.astype(jnp.bfloat16), tokens, preferred_element_type=jnp.float32
    ).astype(jnp.bfloat16)
    sent_scale = jnp.einsum(
        "tks,tk->s", placed, route_weight.astype(jnp.float32), precision=lax.Precision.HIGHEST
    ).astype(jnp.bfloat16)
    sent = jnp.concatenate(
        [sent_rows, jnp.broadcast_to(sent_scale[:, None], (slot_count, 128))], axis=1
    ).reshape(n_expert, slots_cap, feat_part + 128)
    came = []
    for step in range(n_expert):
        block = lax.dynamic_index_in_dim(sent, lax.rem(my_expert + step, n_expert), 0, keepdims=False)
        came.append(lax.ppermute(block, "expert", shift_by("expert", step)) if step else block)
    came = jnp.stack(came)
    slots = jnp.concatenate(
        [
            lax.dynamic_index_in_dim(came, lax.rem(my_expert - group + n_expert, n_expert), 0, keepdims=False)
            for group in range(n_expert)
        ],
        axis=0,
    )
    scale = slots[:, feat_part : feat_part + 1].astype(jnp.float32)
    rows_full = gather_rows(slots[:, :feat_part])
    rows = jnp.concatenate(
        [lax.dynamic_slice(rows_full, (0, start), (slot_count, depth)) for start in order], axis=1
    )
    grad_rows = grad_hidden.reshape(slot_count, hidden_part)

    n_chunk = len(chunks)
    own_at = OWN_AT
    for chunk in range(n_chunk):
        for later in range(1, n_chunk):
            if own_at[later] == chunk:
                to_owner(later, 0)
                to_both(later, 0)
        if chunk:
            for step in shifts:
                to_owner(chunk, step)
        for step in shifts:
            to_both(chunk, step)
        parts = []
        for step in range(n_expert):
            parts += [landed[chunk, step], spread[chunk, step]] if pair else [spread[chunk, step]]
        *carried, done = expert_chunk(rows, scale, grad_rows, parts, chunks[chunk][0], carried)
        finished.append(done)
    hidden, back = carried

    blocks_per_part = feat_part // depth

    def features(part_index):
        blocks = []
        for block in range(blocks_per_part):
            number = part_index * blocks_per_part + block
            start = place_of(number // n_expert, lax.rem(number, n_expert))
            blocks.append(lax.dynamic_slice(back, (0, start), (slot_count, depth)))
        return jnp.concatenate(blocks, axis=1)

    sums = {bits: features(my_mp ^ bits) for bits in range(n_mp)}
    bit = 1
    while 2 * bit < n_mp:
        going = [bits for bits in sums if bits & bit]
        got = lax.ppermute(jnp.stack([sums[bits] for bits in going]), "mp", exchange("mp", bit))
        for index, bits in enumerate(going):
            sums[bits ^ bit] = sums[bits ^ bit] + got[index]
            del sums[bits]
        bit *= 2
    kept = sums[0].reshape(n_expert, slots_cap, feat_part)
    given = sums[bit].reshape(n_expert, slots_cap, feat_part)
    returned = {}
    far_first = sorted(range(n_expert), key=lambda s: abs(2 * s - n_expert) if s else 2 * n_expert)
    bunch = n_expert // Y_PARTS
    for turn in range(0, n_expert, bunch):
        steps = far_first[turn : turn + bunch]
        groups = [lax.rem(my_expert + step, n_expert) for step in steps]
        pick = lambda blocks: jnp.stack(
            [lax.dynamic_index_in_dim(blocks, group, 0, keepdims=False) for group in groups]
        )
        came_back = lax.ppermute(pick(given).astype(jnp.bfloat16), "mp", exchange("mp", bit))
        summed = (pick(kept) + came_back.astype(jnp.float32)).astype(jnp.bfloat16)
        for index, step in enumerate(steps):
            block = summed[index]
            returned[step] = lax.ppermute(block, "expert", shift_by("expert", step)) if step else block
    split = select.reshape(select.shape[0], n_expert, slots_cap)
    chosen = jnp.concatenate(
        [
            lax.dynamic_index_in_dim(split, lax.rem(my_expert - step + n_expert, n_expert), 1, keepdims=False)
            for step in range(n_expert)
        ],
        axis=1,
    )
    grad_tokens = jnp.dot(
        chosen,
        jnp.concatenate([returned[step] for step in range(n_expert)], axis=0).astype(jnp.float32),
        precision=lax.Precision.HIGHEST,
    )
    hidden_out = hidden.reshape(1, 1, n_expert, slots_cap, hidden_part)
    return (hidden_out, grad_tokens.astype(jnp.bfloat16))


def solution(mesh):
    in_specs = (
        P(("dp", "expert"), "mp"),
        P(("dp", "expert"), None),
        P(("dp", "expert"), None),
        P(None, ("dp", "expert"), "mp"),
        P(None, ("dp", "expert"), "mp"),
        P("expert", "dp", None, None, "mp"),
    )
    out_specs = (P("expert", "dp", None, None, "mp"), P(("dp", "expert"), "mp"))
    return jax.shard_map(
        per_device, mesh=mesh, in_specs=in_specs, out_specs=out_specs, check_vma=False
    )
```

```python
import functools

import jax
import jax.numpy as jnp
from jax import lax
from jax.experimental import pallas as pl
from jax.experimental.pallas import tpu as pltpu
from jax.sharding import PartitionSpec as P

Z_WINDOW = 3
X_WINDOW = 3
Z_AFTER = {3: 0, 4: 1}
X_AFTER = {2: 0, 3: 1, 4: 2}
OWN_AT = (0, 0, 0, 1, 2, 3, 4, 5)
Y_PARTS = 2
NT = (((1,), (1,)), ((), ()))


def slot_map(expert_ids, n_expert, slots_cap):
    flat_ids = expert_ids.reshape(-1)
    onehot = (flat_ids[:, None] == jnp.arange(n_expert, dtype=jnp.int32)[None, :]).astype(jnp.int32)
    before = jnp.cumsum(onehot, axis=0) - onehot
    position = jnp.sum(before * onehot, axis=1)
    target = flat_ids * slots_cap + position
    placed = target[:, None] == jnp.arange(n_expert * slots_cap, dtype=jnp.int32)[None, :]
    return placed.reshape(expert_ids.shape[0], expert_ids.shape[1], n_expert * slots_cap)


def shift_by(axis, step):
    size = lax.axis_size(axis)
    return [(source, (source + step) % size) for source in range(size)]


def exchange(axis, bit):
    return [(source, source ^ bit) for source in range(lax.axis_size(axis))]


def after(value, *others):
    return lax.optimization_barrier((value, *others))[0]


def gather_rows(block):
    size = lax.axis_size("mp")
    me = lax.axis_index("mp")
    held = jnp.stack([block] + [lax.ppermute(block, "mp", exchange("mp", bits)) for bits in range(1, size)])
    return jnp.concatenate([lax.dynamic_index_in_dim(held, me ^ index, 0, keepdims=False) for index in range(size)], axis=1)


def column_chunks(width):
    unit = width // 16
    places = ((0, 3), (6, 4), (10, 4), (3, 3), (14, 2))
    return [(begin * unit, (begin + size) * unit) for begin, size in places]


def expert_kernel(n_part, first, rows_ref, scale_ref, grad_ref, *refs):
    parts, rest = refs[:n_part], refs[n_part:]
    if first:
        hidden_ref, back_ref, done_ref = rest
    else:
        back_in, _, hidden_ref, back_ref, done_ref = rest
    depth = parts[0].shape[1]

    @pl.when(pl.program_id(0) == 0)
    def _():
        if first:
            back_ref[...] = jnp.zeros_like(back_ref)
        else:
            back_ref[...] = back_in[...]
        done_ref[...] = jnp.zeros_like(done_ref)

    gate = up = None
    for index, part in enumerate(parts):
        rows = rows_ref[:, index * depth : (index + 1) * depth]
        gate_term = jnp.dot(rows, part[0], preferred_element_type=jnp.float32)
        up_term = jnp.dot(rows, part[1], preferred_element_type=jnp.float32)
        gate = gate_term if gate is None else gate + gate_term
        up = up_term if up is None else up + up_term
    weight = scale_ref[...]
    sig = jax.nn.sigmoid(gate)
    hidden_ref[...] = (weight * gate * sig * up).astype(jnp.bfloat16)
    grad_act = weight * grad_ref[...].astype(jnp.float32)
    gate_grad = (grad_act * up * sig * (1.0 + gate * (1.0 - sig))).astype(jnp.bfloat16)
    up_grad = (grad_act * gate * sig).astype(jnp.bfloat16)
    for index, part in enumerate(parts):
        columns = slice(index * depth, (index + 1) * depth)
        back_ref[:, columns] += lax.dot_general(
            gate_grad, part[0], NT, preferred_element_type=jnp.float32
        ) + lax.dot_general(up_grad, part[1], NT, preferred_element_type=jnp.float32)


def expert_chunk(rows, scale, grad, parts, begin, carried):
    slot_count, width_all = rows.shape
    hidden_part = grad.shape[1]
    depth, width = parts[0].shape[1:]
    tile = 256 if width % 256 == 0 and begin % 256 == 0 else 128
    tile = width if width < 512 and begin % width == 0 else tile
    tile = tile if width % tile == 0 else width
    offset = begin // tile
    whole = lambda shape: pl.BlockSpec(shape, lambda t: (0, 0))
    columns = pl.BlockSpec((slot_count, tile), lambda t: (0, offset + t))
    in_specs = [whole((slot_count, width_all)), whole((slot_count, 1)), columns]
    in_specs += [pl.BlockSpec((2, depth, tile), lambda t: (0, 0, t))] * len(parts)
    operands = [rows, scale, grad, *parts]
    aliases = {}
    if carried is not None:
        hidden, back = carried
        in_specs += [whole((slot_count, width_all)), pl.BlockSpec(memory_space=pl.ANY)]
        aliases = {len(operands): 1, len(operands) + 1: 0}
        operands += [back, hidden]
    return pl.pallas_call(
        functools.partial(expert_kernel, len(parts), carried is None),
        grid=(width // tile,),
        out_shape=(
            jax.ShapeDtypeStruct((slot_count, hidden_part), jnp.bfloat16),
            jax.ShapeDtypeStruct((slot_count, width_all), jnp.float32),
            jax.ShapeDtypeStruct((8, 128), jnp.float32),
        ),
        in_specs=in_specs,
        out_specs=(columns, whole((slot_count, width_all)), whole((8, 128))),
        input_output_aliases=aliases,
        compiler_params=pltpu.CompilerParams(vmem_limit_bytes=48 * 1024 * 1024),
        cost_estimate=pl.CostEstimate(
            flops=1024, bytes_accessed=1024, transcendentals=0,
        ),
    )(*operands)


def per_device(tokens, expert_ids, route_weight, w_gate, w_up, grad_hidden):
    n_expert = lax.axis_size("expert")
    n_dp = lax.axis_size("dp")
    n_mp = lax.axis_size("mp")
    my_expert = lax.axis_index("expert")
    my_dp = lax.axis_index("dp")
    my_mp = lax.axis_index("mp")
    slots_cap = grad_hidden.shape[3]
    feat_part = tokens.shape[1]
    depth = w_gate.shape[1]
    hidden_part = w_gate.shape[2]
    slot_count = n_expert * slots_cap
    width_all = n_expert * n_dp * depth
    chunks = column_chunks(hidden_part)
    pair = n_dp == 2

    def stored(chunk, step):
        begin, end = chunks[chunk]
        target = lax.rem(my_expert + step, n_expert)
        return jnp.stack(
            [
                lax.dynamic_slice(w, (target, 0, begin), (1, depth, end - begin))[0]
                for w in (w_gate, w_up)
            ]
        )

    shifts = sorted(range(1, n_expert), key=lambda s: -abs(2 * s - n_expert))
    landed, arrivals = {}, []
    spread, crossings = {}, []
    carried, finished = None, []

    def to_owner(chunk, step):
        piece = stored(chunk, step)
        if step:
            first = [arrivals[-Z_WINDOW]] if len(arrivals) >= Z_WINDOW else []
            if chunk in Z_AFTER:
                first.append(finished[Z_AFTER[chunk]])
            if first:
                piece = after(piece, *first)
            piece = lax.ppermute(piece, "expert", shift_by("expert", step))
            arrivals.append(piece)
        landed[chunk, step] = piece

    def to_both(chunk, step):
        piece = landed[chunk, step]
        first = [crossings[-X_WINDOW]] if len(crossings) >= X_WINDOW else []
        if step and chunk in X_AFTER:
            first.append(finished[X_AFTER[chunk]])
        if first:
            piece = after(piece, *first)
        if pair:
            spread[chunk, step] = lax.ppermute(piece, "dp", shift_by("dp", 1))
        else:
            spread[chunk, step] = lax.all_gather(piece, "dp", axis=1, tiled=True)
        crossings.append(spread[chunk, step])

    to_owner(0, 0)
    for step in shifts:
        to_owner(0, step)
    to_both(0, 0)

    def place_of(dp_index, expert_index):
        step = lax.rem(my_expert - expert_index + n_expert, n_expert)
        far = lax.rem(my_dp - dp_index + n_dp, n_dp) if pair else dp_index
        return (step * n_dp + far) * depth

    order = []
    for step in range(n_expert):
        expert_index = lax.rem(my_expert - step + n_expert, n_expert)
        for far in range(n_dp):
            dp_index = lax.rem(my_dp - far + n_dp, n_dp) if pair else far
            order.append((dp_index * n_expert + expert_index) * depth)

    placed = slot_map(expert_ids, n_expert, slots_cap).astype(jnp.float32)
    select = jnp.sum(placed, axis=1)
    sent_rows = jnp.dot(
        select.T.astype(jnp.bfloat16), tokens, preferred_element_type=jnp.float32
    ).astype(jnp.bfloat16)
    sent_scale = jnp.einsum(
        "tks,tk->s", placed, route_weight.astype(jnp.float32), precision=lax.Precision.HIGHEST
    ).astype(jnp.bfloat16)
    sent = jnp.concatenate(
        [sent_rows, jnp.broadcast_to(sent_scale[:, None], (slot_count, 128))], axis=1
    ).reshape(n_expert, slots_cap, feat_part + 128)
    came = []
    for step in range(n_expert):
        block = lax.dynamic_index_in_dim(sent, lax.rem(my_expert + step, n_expert), 0, keepdims=False)
        came.append(lax.ppermute(block, "expert", shift_by("expert", step)) if step else block)
    came = jnp.stack(came)
    slots = jnp.concatenate(
        [
            lax.dynamic_index_in_dim(came, lax.rem(my_expert - group + n_expert, n_expert), 0, keepdims=False)
            for group in range(n_expert)
        ],
        axis=0,
    )
    scale = slots[:, feat_part : feat_part + 1].astype(jnp.float32)
    rows_full = gather_rows(slots[:, :feat_part])
    rows = jnp.concatenate(
        [lax.dynamic_slice(rows_full, (0, start), (slot_count, depth)) for start in order], axis=1
    )
    grad_rows = grad_hidden.reshape(slot_count, hidden_part)

    n_chunk = len(chunks)
    own_at = OWN_AT
    for chunk in range(n_chunk):
        for later in range(1, n_chunk):
            if own_at[later] == chunk:
                to_owner(later, 0)
                to_both(later, 0)
        if chunk:
            for step in shifts:
                to_owner(chunk, step)
        for step in shifts:
            to_both(chunk, step)
        parts = []
        for step in range(n_expert):
            parts += [landed[chunk, step], spread[chunk, step]] if pair else [spread[chunk, step]]
        *carried, done = expert_chunk(rows, scale, grad_rows, parts, chunks[chunk][0], carried)
        finished.append(done)
    hidden, back = carried

    blocks_per_part = feat_part // depth

    def features(part_index):
        blocks = []
        for block in range(blocks_per_part):
            number = part_index * blocks_per_part + block
            start = place_of(number // n_expert, lax.rem(number, n_expert))
            blocks.append(lax.dynamic_slice(back, (0, start), (slot_count, depth)))
        return jnp.concatenate(blocks, axis=1)

    sums = {bits: features(my_mp ^ bits) for bits in range(n_mp)}
    bit = 1
    while 2 * bit < n_mp:
        going = [bits for bits in sums if bits & bit]
        got = lax.ppermute(jnp.stack([sums[bits] for bits in going]), "mp", exchange("mp", bit))
        for index, bits in enumerate(going):
            sums[bits ^ bit] = sums[bits ^ bit] + got[index]
            del sums[bits]
        bit *= 2
    kept = sums[0].reshape(n_expert, slots_cap, feat_part)
    given = sums[bit].reshape(n_expert, slots_cap, feat_part)
    returned = {}
    far_first = sorted(range(n_expert), key=lambda s: abs(2 * s - n_expert) if s else 2 * n_expert)
    bunch = n_expert // Y_PARTS
    for turn in range(0, n_expert, bunch):
        steps = far_first[turn : turn + bunch]
        groups = [lax.rem(my_expert + step, n_expert) for step in steps]
        pick = lambda blocks: jnp.stack(
            [lax.dynamic_index_in_dim(blocks, group, 0, keepdims=False) for group in groups]
        )
        came_back = lax.ppermute(pick(given).astype(jnp.bfloat16), "mp", exchange("mp", bit))
        summed = (pick(kept) + came_back.astype(jnp.float32)).astype(jnp.bfloat16)
        for index, step in enumerate(steps):
            block = summed[index]
            returned[step] = lax.ppermute(block, "expert", shift_by("expert", step)) if step else block
    split = select.reshape(select.shape[0], n_expert, slots_cap)
    chosen = jnp.concatenate(
        [
            lax.dynamic_index_in_dim(split, lax.rem(my_expert - step + n_expert, n_expert), 1, keepdims=False)
            for step in range(n_expert)
        ],
        axis=1,
    )
    grad_tokens = jnp.dot(
        chosen,
        jnp.concatenate([returned[step] for step in range(n_expert)], axis=0).astype(jnp.float32),
        precision=lax.Precision.HIGHEST,
    )
    hidden_out = hidden.reshape(1, 1, n_expert, slots_cap, hidden_part)
    return (hidden_out, grad_tokens.astype(jnp.bfloat16))


def solution(mesh):
    in_specs = (
        P(("dp", "expert"), "mp"),
        P(("dp", "expert"), None),
        P(("dp", "expert"), None),
        P(None, ("dp", "expert"), "mp"),
        P(None, ("dp", "expert"), "mp"),
        P("expert", "dp", None, None, "mp"),
    )
    out_specs = (P("expert", "dp", None, None, "mp"), P(("dp", "expert"), "mp"))
    return jax.shard_map(
        per_device, mesh=mesh, in_specs=in_specs, out_specs=out_specs, check_vma=False
    )
```
